1024 devices in a mesh: tens: 32 (over z), mat: 8 (over y, core), rep: 4 (over x).
Axes of the slice: x: 4, y: 4, z: 32, core: 2. Of those that a mesh axis runs over, the one named last changes fastest.
Arguments:
- integrals: bfloat16 [512, 512, 512], P(('tens', 'rep')), may hold values from -6 to 6
- block_mask: int32 [512, 4, 4], P(('tens', 'rep')), may hold values 0 or 1
- green_occ: bfloat16 [512, 512], replicated, may hold values from -0.25 to 0.25
- green_virt: bfloat16 [512, 512], P(None, 'mat'), may hold values from -0.25 to 0.25
Outputs:
- polar: float32 [512, 512], P(('tens', 'rep'), 'mat')
The draws below stay inside these ranges and needn't reach their ends.
All inputs are finite; a program needn't handle non-finite values. No bound on the sum of `block_mask` on one device may be relied on, other than what follows from the above.
Results may differ from the reference program's by a relative error of at most 0.0041.
Values may be sent and summed in bfloat16 or wider, within the bound.
No kernel may reach another device: no remote copies, remote signals or barrier semaphores. Data moves between devices by JAX's collectives and lax.ppermute only.
A program may use at most 32 MiB of HBM per device.

```python
import jax
import jax.numpy as jnp
from jax import lax

BLK = 128
NBLK = 4
NAO = 512
NAUX = 512


def touch_ends(drawn, own_key, least, high):
    spot = [jax.random.randint(jax.random.fold_in(own_key, axis), (), 0, length) for axis, length in enumerate(drawn.shape)]
    longest = drawn.shape.index(max(drawn.shape))
    next_to = spot[:longest] + [(spot[longest] + 1) % drawn.shape[longest]] + spot[longest + 1:]
    return drawn.at[tuple(spot)].set(least).at[tuple(next_to)].set(high)


def block_levels(stream_key, shape, cuts, smallest, high):
    factor_of, own = 1.0, jax.random.fold_in(stream_key, 6)
    for position, blocks in cuts:
        draws = jnp.exp(jax.random.uniform(jax.random.fold_in(own, position), (blocks,), jnp.float32, smallest / len(cuts), high / len(cuts)))
        factor_of = factor_of * jnp.repeat(draws, shape[position] // blocks).reshape([-1 if axis == position else 1 for axis in range(len(shape))])
    return factor_of


def bell_draw(rng, shape, spread, bound, shards=(), kind=jnp.bfloat16):
    level = block_levels(rng, shape, shards, -0.22, 0.18) if shards else 1.0
    values = jax.random.normal(rng, shape, jnp.float32) * spread * level
    return jnp.minimum(jnp.maximum(values, -bound), bound).astype(kind)


def setup_inputs(seed: int = 0) -> dict:
    splits = jax.random.split(jax.random.key(seed), 5)
    integrals = bell_draw(splits[0], (NAUX, NAO, NAO), 1.0, 6.0, ((0, 128),))
    block_mask = touch_ends((jax.random.randint(splits[1], (NAUX, NBLK, NBLK), 0, 4) < 3).astype(jnp.int32), jax.random.fold_in(splits[1], 1), 0, 1)
    green_occ = bell_draw(splits[2], (NAO, NAO), NAO ** -0.5, 0.25)
    green_virt = bell_draw(splits[3], (NAO, NAO), NAO ** -0.5, 0.25, ((1, 8),))
    return dict(integrals=integrals, block_mask=block_mask, green_occ=green_occ, green_virt=green_virt)


def expand_mask(block_mask, width):
    return jnp.repeat(jnp.repeat(block_mask, width, axis=1), width, axis=2)


def reference(integrals, block_mask, green_occ, green_virt):
    masked = integrals * expand_mask(block_mask, BLK).astype(integrals.dtype)

    def dress_one(slab):
        half = jnp.dot(slab, green_virt, preferred_element_type=jnp.float32).astype(jnp.bfloat16)
        return jnp.dot(green_occ.T, half, preferred_element_type=jnp.float32).astype(jnp.bfloat16)

    dressed = lax.map(dress_one, masked)
    flat_dressed = dressed.reshape(NAUX, NAO * NAO)
    flat_masked = masked.reshape(NAUX, NAO * NAO)
    polar = jnp.dot(flat_dressed, flat_masked.T, preferred_element_type=jnp.float32)
    return polar * jnp.float32(1.0 / NAO)
```

```python
import jax
import jax.numpy as jnp
from jax import lax
from jax.experimental import pallas as pl
from jax.experimental.pallas import tpu as pltpu
from jax.sharding import PartitionSpec as P

BF = jnp.bfloat16
F32 = jnp.float32
NT = (((1,), (1,)), ((), ()))
LIMIT = pltpu.CompilerParams(vmem_limit_bytes=32 * 1024 * 1024)


def one_hot(rows, cols, column_of):
    row = lax.broadcasted_iota(jnp.int32, (rows, 1), 0)
    col = lax.broadcasted_iota(jnp.int32, (rows, cols), 1)
    return jnp.where(column_of(row) == col, 1.0, 0.0).astype(BF)


def dress_kernel(
    mask_hbm, virt_hbm, occ_hbm, slab_hbm, out_ref,
    mask_ref, left_ref, occ_ref, slab_ref, half_ref, rows_ref, sems,
):
    auxs, total, _ = slab_ref.shape
    blocks = mask_ref.shape[1]
    width = total // blocks
    cols = virt_hbm.shape[0]
    first = [
        pltpu.make_async_copy(mask_hbm, mask_ref, sems.at[0]),
        pltpu.make_async_copy(virt_hbm, left_ref.at[pl.ds(0, cols)], sems.at[1]),
    ]
    slabs = [
        pltpu.make_async_copy(slab_hbm.at[a], slab_ref.at[a], sems.at[3 + a]) for a in range(auxs)
    ]
    occ = pltpu.make_async_copy(occ_hbm, occ_ref, sems.at[2])
    for copy in first + slabs + [occ]:
        copy.start()

    start = lax.axis_index("mat") * cols
    left_ref[cols:, :] = one_hot(cols, total, lambda row: row + start)
    height = rows_ref.shape[0]
    kinds = height // cols
    order = one_hot(height, height, lambda row: (row % kinds) * cols + row // kinds)
    lane_block = lax.broadcasted_iota(jnp.int32, (1, total), 1) // width

    for copy in first:
        copy.wait()
    for a in range(auxs):
        slabs[a].wait()
        for b in range(0, blocks, 2):
            strips = []
            for row in (b, b + 1):
                kept = mask_ref[a, row : row + 1, :].astype(F32)
                factor = jnp.zeros((1, total), F32)
                for c in range(blocks):
                    factor = jnp.where(lane_block == c, kept[:, c : c + 1], factor)
                strips.append(slab_ref[a, row * width : (row + 1) * width, :] * factor.astype(BF))
            strip = jnp.concatenate(strips, axis=0)
            at = slice(b * width, (b + 2) * width)
            both = lax.dot_general(left_ref[...], strip, NT, preferred_element_type=F32).astype(BF)
            half_ref[a * cols : (a + 1) * cols, at] = both[:cols]
            rows_ref[(auxs + a) * cols : (auxs + a + 1) * cols, at] = both[cols:]
    occ.wait()
    rows_ref[: auxs * cols, :] = jnp.dot(
        half_ref[...], occ_ref[...], preferred_element_type=F32
    ).astype(BF)
    sorted_rows = jnp.dot(order, rows_ref[...], preferred_element_type=F32).astype(BF)
    parts, lanes = out_ref.shape[0], out_ref.shape[2]
    for h in range(parts):
        out_ref[h] = sorted_rows[:, h * lanes : (h + 1) * lanes]


def pair_kernel(tens_count, rep_count, folds, scale, got_ref, out_ref):
    height = got_ref.shape[0]
    kinds = height // (tens_count * rep_count)
    aux = kinds // 2
    total = height // 2
    per_rep = tens_count * aux

    low_count = aux // folds

    def dressed_row(row):
        r, rest = row // per_rep, row % per_rep
        high, rest = rest // (tens_count * low_count), rest % (tens_count * low_count)
        t, low = rest // low_count, rest % low_count
        return (t * rep_count + r) * kinds + high * low_count + low

    def masked_row(row):
        return (row // aux) * kinds + aux + row % aux

    got = got_ref[...]
    dressed = jnp.dot(
        one_hot(total, height, dressed_row), got, preferred_element_type=F32
    ).astype(BF)
    masked = jnp.dot(
        one_hot(total, height, masked_row), got, preferred_element_type=F32
    ).astype(BF)
    groups, cols, lanes = out_ref.shape
    for m in range(groups // rep_count):
        strip = lax.dot_general(
            masked[m * cols : (m + 1) * cols], dressed, NT, preferred_element_type=F32
        )
        strip = (strip * scale).astype(out_ref.dtype)
        for r in range(rep_count):
            out_ref[m * rep_count + r] = strip[:, r * lanes : (r + 1) * lanes]


def plane_kernel(got_ref, out_ref):
    total = got_ref[0].astype(F32)
    for k in range(1, got_ref.shape[0]):
        total = total + got_ref[k].astype(F32)
    rows = out_ref.shape[0]
    folds = total.shape[1] // rows
    out_ref[...] = jnp.concatenate(
        [total[:, h * rows : (h + 1) * rows].T for h in range(folds)], axis=1
    )


def own_kernel(got_ref, out_ref):
    total = got_ref[0]
    for k in range(1, got_ref.shape[0]):
        total = total + got_ref[k]
    low_count = total.shape[0]
    auxs, cols = out_ref.shape
    for h in range(auxs // low_count):
        out_ref[h * low_count : (h + 1) * low_count, :] = total[:, h * cols : (h + 1) * cols]


def shards(integrals, block_mask, green_occ, green_virt):
    auxs, total, _ = integrals.shape
    cols = green_virt.shape[1]
    tens_count = lax.axis_size("tens")
    rep_count = lax.axis_size("rep")
    mat_count = lax.axis_size("mat")
    owners = tens_count * rep_count
    kinds = 2 * auxs
    parts = owners // cols
    lanes = total // parts

    hbm = pl.BlockSpec(memory_space=pltpu.HBM)
    send = pl.pallas_call(
        dress_kernel,
        out_shape=jax.ShapeDtypeStruct((parts, cols * kinds, lanes), BF),
        in_specs=[hbm] * 4,
        scratch_shapes=[
            pltpu.VMEM(block_mask.shape, jnp.int32),
            pltpu.VMEM((2 * cols, total), BF),
            pltpu.VMEM((total, total), BF),
            pltpu.VMEM(integrals.shape, BF),
            pltpu.VMEM((auxs * cols, total), BF),
            pltpu.VMEM((kinds * cols, total), BF),
            pltpu.SemaphoreType.DMA((3 + auxs,)),
        ],
        compiler_params=pltpu.CompilerParams(vmem_limit_bytes=56 * 1024 * 1024),
        name="dress",
    )(block_mask, green_virt.T, green_occ, integrals)

    got = lax.all_to_all(
        send.reshape(owners, kinds, lanes), ("tens", "rep"), 0, 0, tiled=True
    )

    folds = min(auxs, max(1, 128 // cols))
    partial = pl.pallas_call(
        lambda *refs: pair_kernel(tens_count, rep_count, folds, 1.0 / total, *refs),
        out_shape=jax.ShapeDtypeStruct((mat_count * rep_count, cols, tens_count * auxs), F32),
        compiler_params=LIMIT,
        name="pair",
    )(got.reshape(owners * kinds, lanes))
    partial = lax.all_to_all(partial, ("mat", "rep"), 0, 0, tiled=True)

    rows = pl.pallas_call(
        plane_kernel,
        out_shape=jax.ShapeDtypeStruct((tens_count * auxs // folds, folds * cols), F32),
        compiler_params=LIMIT,
        name="plane_sum",
    )(partial)
    rows = rows.reshape(tens_count, auxs // folds, folds * cols)
    rows = lax.all_to_all(rows, "tens", 0, 0, tiled=True)
    return pl.pallas_call(
        own_kernel,
        out_shape=jax.ShapeDtypeStruct((auxs, cols), F32),
        compiler_params=LIMIT,
        name="own_sum",
    )(rows)


def solution(mesh):
    return jax.shard_map(
        shards,
        mesh=mesh,
        in_specs=(
            P(("tens", "rep"), None, None),
            P(("tens", "rep"), None, None),
            P(),
            P(None, "mat"),
        ),
        out_specs=P(("tens", "rep"), "mat"),
        check_vma=False,
    )
```

```python
import jax
import jax.numpy as jnp
from jax import lax
from jax.experimental import pallas as pl
from jax.experimental.pallas import tpu as pltpu
from jax.sharding import PartitionSpec as P

BF = jnp.bfloat16
F32 = jnp.float32
NT = (((1,), (1,)), ((), ()))
LIMIT = pltpu.CompilerParams(vmem_limit_bytes=32 * 1024 * 1024)


def one_hot(rows, cols, column_of):
    row = lax.broadcasted_iota(jnp.int32, (rows, 1), 0)
    col = lax.broadcasted_iota(jnp.int32, (rows, cols), 1)
    return jnp.where(column_of(row) == col, 1.0, 0.0).astype(BF)


def dress_kernel(
    mask_hbm, virt_hbm, occ_hbm, slab_hbm, out_ref,
    mask_ref, left_ref, occ_ref, slab_ref, half_ref, rows_ref, sems,
):
    auxs, total, _ = slab_ref.shape
    blocks = mask_ref.shape[1]
    width = total // blocks
    cols = virt_hbm.shape[0]
    first = [
        pltpu.make_async_copy(mask_hbm, mask_ref, sems.at[0]),
        pltpu.make_async_copy(virt_hbm, left_ref.at[pl.ds(0, cols)], sems.at[1]),
    ]
    slabs = [
        pltpu.make_async_copy(slab_hbm.at[a], slab_ref.at[a], sems.at[3 + a]) for a in range(auxs)
    ]
    occ = pltpu.make_async_copy(occ_hbm, occ_ref, sems.at[2])
    for copy in first + slabs + [occ]:
        copy.start()

    start = lax.axis_index("mat") * cols
    left_ref[cols:, :] = one_hot(cols, total, lambda row: row + start)
    height = rows_ref.shape[0]
    kinds = height // cols
    order = one_hot(height, height, lambda row: (row % kinds) * cols + row // kinds)
    lane_block = lax.broadcasted_iota(jnp.int32, (1, total), 1) // width

    for copy in first:
        copy.wait()
    for a in range(auxs):
        slabs[a].wait()
        for b in range(0, blocks, 2):
            strips = []
            for row in (b, b + 1):
                kept = mask_ref[a, row : row + 1, :].astype(F32)
                factor = jnp.zeros((1, total), F32)
                for c in range(blocks):
                    factor = jnp.where(lane_block == c, kept[:, c : c + 1], factor)
                strips.append(slab_ref[a, row * width : (row + 1) * width, :] * factor.astype(BF))
            strip = jnp.concatenate(strips, axis=0)
            at = slice(b * width, (b + 2) * width)
            both = lax.dot_general(left_ref[...], strip, NT, preferred_element_type=F32).astype(BF)
            half_ref[a * cols : (a + 1) * cols, at] = both[:cols]
            rows_ref[(auxs + a) * cols : (auxs + a + 1) * cols, at] = both[cols:]
    occ.wait()
    rows_ref[: auxs * cols, :] = jnp.dot(
        half_ref[...], occ_ref[...], preferred_element_type=F32
    ).astype(BF)
    sorted_rows = jnp.dot(order, rows_ref[...], preferred_element_type=F32).astype(BF)
    parts, lanes = out_ref.shape[0], out_ref.shape[2]
    for h in range(parts):
        out_ref[h] = sorted_rows[:, h * lanes : (h + 1) * lanes]


def pair_kernel(tens_count, rep_count, folds, scale, got_ref, out_ref):
    height = got_ref.shape[0]
    kinds = height // (tens_count * rep_count)
    aux = kinds // 2
    total = height // 2
    per_rep = tens_count * aux

    low_count = aux // folds

    def dressed_row(row):
        r, rest = row // per_rep, row % per_rep
        high, rest = rest // (tens_count * low_count), rest % (tens_count * low_count)
        t, low = rest // low_count, rest % low_count
        return (t * rep_count + r) * kinds + high * low_count + low

    def masked_row(row):
        return (row // aux) * kinds + aux + row % aux

    got = got_ref[...]
    dressed = jnp.dot(
        one_hot(total, height, dressed_row), got, preferred_element_type=F32
    ).astype(BF)
    masked = jnp.dot(
        one_hot(total, height, masked_row), got, preferred_element_type=F32
    ).astype(BF)
    groups, cols, lanes = out_ref.shape
    for m in range(groups // rep_count):
        strip = lax.dot_general(
            masked[m * cols : (m + 1) * cols], dressed, NT, preferred_element_type=F32
        )
        strip = (strip * scale).astype(out_ref.dtype)
        for r in range(rep_count):
            out_ref[m * rep_count + r] = strip[:, r * lanes : (r + 1) * lanes]


def plane_kernel(got_ref, out_ref):
    total = got_ref[0].astype(F32)
    for k in range(1, got_ref.shape[0]):
        total = total + got_ref[k].astype(F32)
    rows = out_ref.shape[0]
    folds = total.shape[1] // rows
    out_ref[...] = jnp.concatenate(
        [total[:, h * rows : (h + 1) * rows].T for h in range(folds)], axis=1
    )


def own_kernel(got_ref, out_ref):
    total = got_ref[0]
    for k in range(1, got_ref.shape[0]):
        total = total + got_ref[k]
    low_count = total.shape[0]
    auxs, cols = out_ref.shape
    for h in range(auxs // low_count):
        out_ref[h * low_count : (h + 1) * low_count, :] = total[:, h * cols : (h + 1) * cols]


def shards(integrals, block_mask, green_occ, green_virt):
    auxs, total, _ = integrals.shape
    cols = green_virt.shape[1]
    tens_count = lax.axis_size("tens")
    rep_count = lax.axis_size("rep")
    mat_count = lax.axis_size("mat")
    owners = tens_count * rep_count
    kinds = 2 * auxs
    parts = owners // cols
    lanes = total // parts

    hbm = pl.BlockSpec(memory_space=pltpu.HBM)
    send = pl.pallas_call(
        dress_kernel,
        out_shape=jax.ShapeDtypeStruct((parts, cols * kinds, lanes), BF),
        in_specs=[hbm] * 4,
        scratch_shapes=[
            pltpu.VMEM(block_mask.shape, jnp.int32),
            pltpu.VMEM((2 * cols, total), BF),
            pltpu.VMEM((total, total), BF),
            pltpu.VMEM(integrals.shape, BF),
            pltpu.VMEM((auxs * cols, total), BF),
            pltpu.VMEM((kinds * cols, total), BF),
            pltpu.SemaphoreType.DMA((3 + auxs,)),
        ],
        compiler_params=pltpu.CompilerParams(vmem_limit_bytes=56 * 1024 * 1024),
        name="dress",
    )(block_mask, green_virt.T, green_occ, integrals)

    got = lax.all_to_all(
        send.reshape(owners, kinds, lanes), ("tens", "rep"), 0, 0, tiled=True
    )

    folds = min(auxs, max(1, 128 // cols))
    partial = pl.pallas_call(
        lambda *refs: pair_kernel(tens_count, rep_count, folds, 1.0 / total, *refs),
        out_shape=jax.ShapeDtypeStruct((mat_count * rep_count, cols, tens_count * auxs), BF),
        compiler_params=LIMIT,
        name="pair",
    )(got.reshape(owners * kinds, lanes))
    partial = lax.all_to_all(partial, ("mat", "rep"), 0, 0, tiled=True)

    rows = pl.pallas_call(
        plane_kernel,
        out_shape=jax.ShapeDtypeStruct((tens_count * auxs // folds, folds * cols), F32),
        compiler_params=LIMIT,
        name="plane_sum",
    )(partial)
    rows = rows.reshape(tens_count, auxs // folds, folds * cols)
    rows = lax.all_to_all(rows, "tens", 0, 0, tiled=True)
    return pl.pallas_call(
        own_kernel,
        out_shape=jax.ShapeDtypeStruct((auxs, cols), F32),
        compiler_params=LIMIT,
        name="own_sum",
    )(rows)


def solution(mesh):
    return jax.shard_map(
        shards,
        mesh=mesh,
        in_specs=(
            P(("tens", "rep"), None, None),
            P(("tens", "rep"), None, None),
            P(),
            P(None, "mat"),
        ),
        out_specs=P(("tens", "rep"), "mat"),
        check_vma=False,
    )
```

```python
import jax
import jax.numpy as jnp
from jax import lax
from jax.experimental import pallas as pl
from jax.experimental.pallas import tpu as pltpu
from jax.sharding import PartitionSpec as P

BF = jnp.bfloat16
F32 = jnp.float32
NT = (((1,), (1,)), ((), ()))
LIMIT = pltpu.CompilerParams(vmem_limit_bytes=32 * 1024 * 1024)


def one_hot(rows, cols, column_of):
    row = lax.broadcasted_iota(jnp.int32, (rows, 1), 0)
    col = lax.broadcasted_iota(jnp.int32, (rows, cols), 1)
    return jnp.where(column_of(row) == col, 1.0, 0.0).astype(BF)


def dress_kernel(
    mask_hbm, virt_hbm, occ_hbm, slab_hbm, out_hbm,
    mask_ref, left_ref, occ_ref, slab_ref, half_ref, rows_ref, out_ref, sems,
):
    auxs, total, _ = slab_ref.shape
    blocks = mask_ref.shape[1]
    width = total // blocks
    cols = virt_hbm.shape[0]
    mask = pltpu.make_async_copy(mask_hbm, mask_ref, sems.at[0])
    virt = pltpu.make_async_copy(virt_hbm, left_ref.at[pl.ds(0, cols)], sems.at[1])
    occ = pltpu.make_async_copy(occ_hbm, occ_ref, sems.at[2])
    slabs = [
        pltpu.make_async_copy(slab_hbm.at[a], slab_ref.at[a], sems.at[3 + a]) for a in range(auxs)
    ]
    for copy in [mask, virt] + slabs[:1] + [occ] + slabs[1:]:
        copy.start()

    start = lax.axis_index("mat") * cols
    left_ref[cols:, :] = one_hot(cols, total, lambda row: row + start)
    kinds = rows_ref.shape[0] // cols
    band = min(cols, 32)
    order = one_hot(
        kinds * band, kinds * band, lambda row: (row % kinds) * band + row // kinds
    )
    lane_block = lax.broadcasted_iota(jnp.int32, (1, total), 1) // width

    mask.wait()
    virt.wait()
    done = 0
    for a in range(auxs):
        slabs[a].wait()
        for b in range(0, blocks, 2):
            strips = []
            for row in (b, b + 1):
                kept = mask_ref[a, row : row + 1, :].astype(F32)
                factor = jnp.zeros((1, total), F32)
                for c in range(blocks):
                    factor = jnp.where(lane_block == c, kept[:, c : c + 1], factor)
                strips.append(slab_ref[a, row * width : (row + 1) * width, :] * factor.astype(BF))
            strip = jnp.concatenate(strips, axis=0)
            at = slice(b * width, (b + 2) * width)
            both = lax.dot_general(left_ref[...], strip, NT, preferred_element_type=F32).astype(BF)
            half_ref[a * cols : (a + 1) * cols, at] = both[:cols]
            rows_ref[(auxs + a) * cols : (auxs + a + 1) * cols, at] = both[cols:]
        if a == 0:
            occ.wait()
        if a % 2 == 1 or a == auxs - 1:
            at = slice(done * cols, (a + 1) * cols)
            rows_ref[at, :] = jnp.dot(
                half_ref[at, :], occ_ref[...], preferred_element_type=F32
            ).astype(BF)
            done = a + 1

    parts, lanes = out_ref.shape[0], out_ref.shape[2]
    outs = []
    for h in range(parts):
        for g in range(cols // band):
            rows = jnp.concatenate(
                [
                    rows_ref[
                        j * cols + g * band : j * cols + (g + 1) * band,
                        h * lanes : (h + 1) * lanes,
                    ]
                    for j in range(kinds)
                ],
                axis=0,
            )
            out_ref[h, g * kinds * band : (g + 1) * kinds * band, :] = jnp.dot(
                order, rows, preferred_element_type=F32
            ).astype(BF)
        copy = pltpu.make_async_copy(out_ref.at[h], out_hbm.at[h], sems.at[3 + auxs + h])
        copy.start()
        outs.append(copy)
    for copy in outs:
        copy.wait()


def pair_kernel(tens_count, rep_count, folds, scale, got_ref, out_ref):
    height = got_ref.shape[0]
    kinds = height // (tens_count * rep_count)
    aux = kinds // 2
    low_count = aux // folds
    near = min(tens_count, max(1, 256 // (rep_count * kinds)))
    rows = near * rep_count * kinds
    piece = near * low_count

    def source_row(row):
        r, rest = row // (near * aux), row % (near * aux)
        high, rest = rest // piece, rest % piece
        t, low = rest // low_count, rest % low_count
        dressed = (t * rep_count + r) * kinds + high * low_count + low
        back = row - rows // 2
        masked = (back // aux) * kinds + aux + back % aux
        return jnp.where(row < rows // 2, dressed, masked)

    order = one_hot(rows, rows, source_row)
    groups = [
        jnp.dot(
            order, got_ref[g * rows : (g + 1) * rows, :], preferred_element_type=F32
        ).astype(BF)
        for g in range(height // rows)
    ]
    dressed = jnp.concatenate(
        [
            group[(r * folds + high) * piece : (r * folds + high + 1) * piece]
            for r in range(rep_count)
            for high in range(folds)
            for group in groups
        ],
        axis=0,
    )
    slots, cols, lanes = out_ref.shape
    for g, group in enumerate(groups):
        block = lax.dot_general(group[rows // 2 :], dressed, NT, preferred_element_type=F32)
        block = (block * scale).astype(out_ref.dtype)
        per = block.shape[0] // cols
        for k in range(per):
            for r in range(rep_count):
                out_ref[(g * per + k) * rep_count + r] = block[
                    k * cols : (k + 1) * cols, r * lanes : (r + 1) * lanes
                ]


def plane_kernel(got_ref, out_ref):
    total = got_ref[0].astype(F32)
    for k in range(1, got_ref.shape[0]):
        total = total + got_ref[k].astype(F32)
    rows = out_ref.shape[0]
    folds = total.shape[1] // rows
    out_ref[...] = jnp.concatenate(
        [total[:, h * rows : (h + 1) * rows].T for h in range(folds)], axis=1
    )


def own_kernel(got_ref, out_ref):
    total = got_ref[0]
    for k in range(1, got_ref.shape[0]):
        total = total + got_ref[k]
    low_count = total.shape[0]
    auxs, cols = out_ref.shape
    for h in range(auxs // low_count):
        out_ref[h * low_count : (h + 1) * low_count, :] = total[:, h * cols : (h + 1) * cols]


def shards(integrals, block_mask, green_occ, green_virt):
    auxs, total, _ = integrals.shape
    cols = green_virt.shape[1]
    tens_count = lax.axis_size("tens")
    rep_count = lax.axis_size("rep")
    mat_count = lax.axis_size("mat")
    owners = tens_count * rep_count
    kinds = 2 * auxs
    parts = owners // cols
    lanes = total // parts

    hbm = pl.BlockSpec(memory_space=pltpu.HBM)
    send = pl.pallas_call(
        dress_kernel,
        out_shape=jax.ShapeDtypeStruct((parts, cols * kinds, lanes), BF),
        in_specs=[hbm] * 4,
        out_specs=hbm,
        scratch_shapes=[
            pltpu.VMEM(block_mask.shape, jnp.int32),
            pltpu.VMEM((2 * cols, total), BF),
            pltpu.VMEM((total, total), BF),
            pltpu.VMEM(integrals.shape, BF),
            pltpu.VMEM((auxs * cols, total), BF),
            pltpu.VMEM((kinds * cols, total), BF),
            pltpu.VMEM((parts, cols * kinds, lanes), BF),
            pltpu.SemaphoreType.DMA((3 + auxs + parts,)),
        ],
        compiler_params=pltpu.CompilerParams(vmem_limit_bytes=56 * 1024 * 1024),
        name="dress",
    )(block_mask, green_virt.T, green_occ, integrals)

    got = lax.all_to_all(
        send.reshape(owners, kinds, lanes), ("tens", "rep"), 0, 0, tiled=True
    )

    folds = min(auxs, max(1, 128 // cols))
    partial = pl.pallas_call(
        lambda *refs: pair_kernel(tens_count, rep_count, folds, 1.0 / total, *refs),
        out_shape=jax.ShapeDtypeStruct((mat_count * rep_count, cols, tens_count * auxs), BF),
        compiler_params=LIMIT,
        name="pair",
    )(got.reshape(owners * kinds, lanes))
    partial = lax.all_to_all(partial, ("mat", "rep"), 0, 0, tiled=True)

    rows = pl.pallas_call(
        plane_kernel,
        out_shape=jax.ShapeDtypeStruct((tens_count * auxs // folds, folds * cols), F32),
        compiler_params=LIMIT,
        name="plane_sum",
    )(partial)
    rows = rows.reshape(tens_count, auxs // folds, folds * cols)
    rows = lax.all_to_all(rows, "tens", 0, 0, tiled=True)
    return pl.pallas_call(
        own_kernel,
        out_shape=jax.ShapeDtypeStruct((auxs, cols), F32),
        compiler_params=LIMIT,
        name="own_sum",
    )(rows)


def solution(mesh):
    return jax.shard_map(
        shards,
        mesh=mesh,
        in_specs=(
            P(("tens", "rep"), None, None),
            P(("tens", "rep"), None, None),
            P(),
            P(None, "mat"),
        ),
        out_specs=P(("tens", "rep"), "mat"),
        check_vma=False,
    )
```

```python
import jax
import jax.numpy as jnp
from jax import lax
from jax.experimental import pallas as pl
from jax.experimental.pallas import tpu as pltpu
from jax.sharding import PartitionSpec as P

BF = jnp.bfloat16
F32 = jnp.float32
NT = (((1,), (1,)), ((), ()))
LIMIT = pltpu.CompilerParams(vmem_limit_bytes=32 * 1024 * 1024)


def one_hot(rows, cols, column_of):
    row = lax.broadcasted_iota(jnp.int32, (rows, 1), 0)
    col = lax.broadcasted_iota(jnp.int32, (rows, cols), 1)
    return jnp.where(column_of(row) == col, 1.0, 0.0).astype(BF)


def dress_kernel(
    mask_hbm, virt_hbm, occ_hbm, slab_hbm, out_ref,
    mask_ref, left_ref, occ_ref, slab_ref, half_ref, rows_ref, sems,
):
    auxs, total, _ = slab_ref.shape
    blocks = mask_ref.shape[1]
    width = total // blocks
    cols = virt_hbm.shape[0]
    mask = pltpu.make_async_copy(mask_hbm, mask_ref, sems.at[0])
    virt = pltpu.make_async_copy(virt_hbm, left_ref.at[pl.ds(0, cols)], sems.at[1])
    occ = pltpu.make_async_copy(occ_hbm, occ_ref, sems.at[2])
    slabs = [
        pltpu.make_async_copy(slab_hbm.at[a], slab_ref.at[a], sems.at[3 + a]) for a in range(auxs)
    ]
    for copy in [mask, virt] + slabs + [occ]:
        copy.start()

    start = lax.axis_index("mat") * cols
    left_ref[cols:, :] = one_hot(cols, total, lambda row: row + start)
    kinds = rows_ref.shape[0] // cols
    band = min(cols, 32)
    order = one_hot(
        kinds * band, kinds * band, lambda row: (row % kinds) * band + row // kinds
    )
    lane_block = lax.broadcasted_iota(jnp.int32, (1, total), 1) // width

    mask.wait()
    virt.wait()
    for a in range(auxs):
        slabs[a].wait()
        for b in range(0, blocks, 2):
            strips = []
            for row in (b, b + 1):
                kept = mask_ref[a, row : row + 1, :].astype(F32)
                factor = jnp.zeros((1, total), F32)
                for c in range(blocks):
                    factor = jnp.where(lane_block == c, kept[:, c : c + 1], factor)
                strips.append(slab_ref[a, row * width : (row + 1) * width, :] * factor.astype(BF))
            strip = jnp.concatenate(strips, axis=0)
            at = slice(b * width, (b + 2) * width)
            both = lax.dot_general(left_ref[...], strip, NT, preferred_element_type=F32).astype(BF)
            half_ref[a * cols : (a + 1) * cols, at] = both[:cols]
            rows_ref[(auxs + a) * cols : (auxs + a + 1) * cols, at] = both[cols:]
    occ.wait()
    rows_ref[: auxs * cols, :] = jnp.dot(
        half_ref[...], occ_ref[...], preferred_element_type=F32
    ).astype(BF)

    parts, lanes = out_ref.shape[0], out_ref.shape[2]
    for h in range(parts):
        for g in range(cols // band):
            rows = jnp.concatenate(
                [
                    rows_ref[
                        j * cols + g * band : j * cols + (g + 1) * band,
                        h * lanes : (h + 1) * lanes,
                    ]
                    for j in range(kinds)
                ],
                axis=0,
            )
            out_ref[h, g * kinds * band : (g + 1) * kinds * band, :] = jnp.dot(
                order, rows, preferred_element_type=F32
            ).astype(BF)


def pair_kernel(tens_count, rep_count, folds, scale, got_ref, out_ref):
    height = got_ref.shape[0]
    kinds = height // (tens_count * rep_count)
    aux = kinds // 2
    low_count = aux // folds
    near = min(tens_count, max(1, 256 // (rep_count * kinds)))
    rows = near * rep_count * kinds
    piece = near * low_count

    def source_row(row):
        r, rest = row // (near * aux), row % (near * aux)
        high, rest = rest // piece, rest % piece
        t, low = rest // low_count, rest % low_count
        dressed = (t * rep_count + r) * kinds + high * low_count + low
        back = row - rows // 2
        masked = (back // aux) * kinds + aux + back % aux
        return jnp.where(row < rows // 2, dressed, masked)

    order = one_hot(rows, rows, source_row)
    groups = [
        jnp.dot(
            order, got_ref[g * rows : (g + 1) * rows, :], preferred_element_type=F32
        ).astype(BF)
        for g in range(height // rows)
    ]
    dressed = jnp.concatenate(
        [
            group[(r * folds + high) * piece : (r * folds + high + 1) * piece]
            for r in range(rep_count)
            for high in range(folds)
            for group in groups
        ],
        axis=0,
    )
    slots, cols, lanes = out_ref.shape
    for g, group in enumerate(groups):
        block = lax.dot_general(group[rows // 2 :], dressed, NT, preferred_element_type=F32)
        block = (block * scale).astype(out_ref.dtype)
        per = block.shape[0] // cols
        for k in range(per):
            for r in range(rep_count):
                out_ref[(g * per + k) * rep_count + r] = block[
                    k * cols : (k + 1) * cols, r * lanes : (r + 1) * lanes
                ]


def plane_kernel(got_ref, out_ref):
    total = got_ref[0].astype(F32)
    for k in range(1, got_ref.shape[0]):
        total = total + got_ref[k].astype(F32)
    rows = out_ref.shape[0]
    folds = total.shape[1] // rows
    out_ref[...] = jnp.concatenate(
        [total[:, h * rows : (h + 1) * rows].T for h in range(folds)], axis=1
    )


def own_kernel(got_ref, out_ref):
    total = got_ref[0]
    for k in range(1, got_ref.shape[0]):
        total = total + got_ref[k]
    low_count = total.shape[0]
    auxs, cols = out_ref.shape
    for h in range(auxs // low_count):
        out_ref[h * low_count : (h + 1) * low_count, :] = total[:, h * cols : (h + 1) * cols]


def shards(integrals, block_mask, green_occ, green_virt):
    auxs, total, _ = integrals.shape
    cols = green_virt.shape[1]
    tens_count = lax.axis_size("tens")
    rep_count = lax.axis_size("rep")
    mat_count = lax.axis_size("mat")
    owners = tens_count * rep_count
    kinds = 2 * auxs
    parts = owners // cols
    lanes = total // parts

    hbm = pl.BlockSpec(memory_space=pltpu.HBM)
    send = pl.pallas_call(
        dress_kernel,
        out_shape=jax.ShapeDtypeStruct((parts, cols * kinds, lanes), BF),
        in_specs=[hbm] * 4,
        scratch_shapes=[
            pltpu.VMEM(block_mask.shape, jnp.int32),
            pltpu.VMEM((2 * cols, total), BF),
            pltpu.VMEM((total, total), BF),
            pltpu.VMEM(integrals.shape, BF),
            pltpu.VMEM((auxs * cols, total), BF),
            pltpu.VMEM((kinds * cols, total), BF),
            pltpu.SemaphoreType.DMA((3 + auxs,)),
        ],
        compiler_params=LIMIT,
        name="dress",
    )(
        *[
            pltpu.with_memory_space_constraint(x, pltpu.HBM)
            for x in (block_mask, green_virt.T, green_occ, integrals)
        ]
    )

    got = lax.all_to_all(
        send.reshape(owners, kinds, lanes), ("tens", "rep"), 0, 0, tiled=True
    )

    folds = min(auxs, max(1, 128 // cols))
    partial = pl.pallas_call(
        lambda *refs: pair_kernel(tens_count, rep_count, folds, 1.0 / total, *refs),
        out_shape=jax.ShapeDtypeStruct((mat_count * rep_count, cols, tens_count * auxs), BF),
        compiler_params=LIMIT,
        name="pair",
    )(got.reshape(owners * kinds, lanes))
    partial = lax.all_to_all(partial, ("mat", "rep"), 0, 0, tiled=True)

    rows = pl.pallas_call(
        plane_kernel,
        out_shape=jax.ShapeDtypeStruct((tens_count * auxs // folds, folds * cols), F32),
        compiler_params=LIMIT,
        name="plane_sum",
    )(partial)
    rows = rows.reshape(tens_count, auxs // folds, folds * cols)
    rows = lax.all_to_all(rows, "tens", 0, 0, tiled=True)
    return pl.pallas_call(
        own_kernel,
        out_shape=jax.ShapeDtypeStruct((auxs, cols), F32),
        compiler_params=LIMIT,
        name="own_sum",
    )(rows)


def solution(mesh):
    return jax.shard_map(
        shards,
        mesh=mesh,
        in_specs=(
            P(("tens", "rep"), None, None),
            P(("tens", "rep"), None, None),
            P(),
            P(None, "mat"),
        ),
        out_specs=P(("tens", "rep"), "mat"),
        check_vma=False,
    )
```

```python
import jax
import jax.numpy as jnp
from jax import lax
from jax.experimental import pallas as pl
from jax.experimental.pallas import tpu as pltpu
from jax.sharding import PartitionSpec as P

BF = jnp.bfloat16
F32 = jnp.float32
NT = (((1,), (1,)), ((), ()))
LIMIT = pltpu.CompilerParams(vmem_limit_bytes=32 * 1024 * 1024)


def one_hot(rows, cols, column_of):
    row = lax.broadcasted_iota(jnp.int32, (rows, 1), 0)
    col = lax.broadcasted_iota(jnp.int32, (rows, cols), 1)
    return jnp.where(column_of(row) == col, 1.0, 0.0).astype(BF)


def dress_kernel(
    mask_hbm, virt_hbm, occ_hbm, slab_hbm, out_ref,
    mask_ref, left_ref, occ_ref, slab_ref, half_ref, rows_ref, sems,
):
    auxs, total, _ = slab_ref.shape
    blocks = mask_ref.shape[1]
    width = total // blocks
    cols = virt_hbm.shape[0]
    mask = pltpu.make_async_copy(mask_hbm, mask_ref, sems.at[0])
    virt = pltpu.make_async_copy(virt_hbm, left_ref.at[pl.ds(0, cols)], sems.at[1])
    occ = pltpu.make_async_copy(occ_hbm, occ_ref, sems.at[2])
    slabs = [
        pltpu.make_async_copy(slab_hbm.at[a], slab_ref.at[a], sems.at[3 + a]) for a in range(auxs)
    ]
    for copy in slabs[:1] + [mask, virt] + slabs[1:] + [occ]:
        copy.start()

    start = lax.axis_index("mat") * cols
    left_ref[cols:, :] = one_hot(cols, total, lambda row: row + start)
    kinds = rows_ref.shape[0] // cols
    band = min(cols, 32)
    order = one_hot(
        kinds * band, kinds * band, lambda row: (row % kinds) * band + row // kinds
    )
    lane_block = lax.broadcasted_iota(jnp.int32, (1, total), 1) // width

    mask.wait()
    factors = []
    for a in range(auxs):
        for row in range(blocks):
            kept = mask_ref[a, row : row + 1, :].astype(F32)
            factor = jnp.zeros((1, total), F32)
            for c in range(blocks):
                factor = jnp.where(lane_block == c, kept[:, c : c + 1], factor)
            factors.append(factor.astype(BF))
    virt.wait()
    for a in range(auxs):
        slabs[a].wait()
        for b in range(0, blocks, 2):
            strips = []
            for row in (b, b + 1):
                strip = slab_ref[a, row * width : (row + 1) * width, :]
                strips.append(strip * factors[a * blocks + row])
            strip = jnp.concatenate(strips, axis=0)
            at = slice(b * width, (b + 2) * width)
            both = lax.dot_general(left_ref[...], strip, NT, preferred_element_type=F32).astype(BF)
            half_ref[a * cols : (a + 1) * cols, at] = both[:cols]
            rows_ref[(auxs + a) * cols : (auxs + a + 1) * cols, at] = both[cols:]
    occ.wait()
    rows_ref[: auxs * cols, :] = jnp.dot(
        half_ref[...], occ_ref[...], preferred_element_type=F32
    ).astype(BF)

    parts, lanes = out_ref.shape[0], out_ref.shape[2]
    for h in range(parts):
        for g in range(cols // band):
            rows = jnp.concatenate(
                [
                    rows_ref[
                        j * cols + g * band : j * cols + (g + 1) * band,
                        h * lanes : (h + 1) * lanes,
                    ]
                    for j in range(kinds)
                ],
                axis=0,
            )
            out_ref[h, g * kinds * band : (g + 1) * kinds * band, :] = jnp.dot(
                order, rows, preferred_element_type=F32
            ).astype(BF)


def pair_kernel(tens_count, rep_count, folds, scale, got_ref, out_ref):
    height = got_ref.shape[0]
    kinds = height // (tens_count * rep_count)
    aux = kinds // 2
    low_count = aux // folds
    near = min(tens_count, max(1, 256 // (rep_count * kinds)))
    rows = near * rep_count * kinds
    piece = near * low_count

    def source_row(row):
        r, rest = row // (near * aux), row % (near * aux)
        high, rest = rest // piece, rest % piece
        t, low = rest // low_count, rest % low_count
        dressed = (t * rep_count + r) * kinds + high * low_count + low
        back = row - rows // 2
        masked = (back // aux) * kinds + aux + back % aux
        return jnp.where(row < rows // 2, dressed, masked)

    order = one_hot(rows, rows, source_row)
    groups = [
        jnp.dot(
            order, got_ref[g * rows : (g + 1) * rows, :], preferred_element_type=F32
        ).astype(BF)
        for g in range(height // rows)
    ]
    dressed = jnp.concatenate(
        [
            group[(r * folds + high) * piece : (r * folds + high + 1) * piece]
            for r in range(rep_count)
            for high in range(folds)
            for group in groups
        ],
        axis=0,
    )
    slots, cols, lanes = out_ref.shape
    for g, group in enumerate(groups):
        block = lax.dot_general(group[rows // 2 :], dressed, NT, preferred_element_type=F32)
        block = (block * scale).astype(out_ref.dtype)
        per = block.shape[0] // cols
        for k in range(per):
            for r in range(rep_count):
                out_ref[(g * per + k) * rep_count + r] = block[
                    k * cols : (k + 1) * cols, r * lanes : (r + 1) * lanes
                ]


def plane_kernel(got_ref, out_ref):
    total = got_ref[0].astype(F32)
    for k in range(1, got_ref.shape[0]):
        total = total + got_ref[k].astype(F32)
    rows = out_ref.shape[0]
    folds = total.shape[1] // rows
    out_ref[...] = jnp.concatenate(
        [total[:, h * rows : (h + 1) * rows].T for h in range(folds)], axis=1
    )


def own_kernel(got_ref, out_ref):
    total = got_ref[0]
    for k in range(1, got_ref.shape[0]):
        total = total + got_ref[k]
    low_count = total.shape[0]
    auxs, cols = out_ref.shape
    for h in range(auxs // low_count):
        out_ref[h * low_count : (h + 1) * low_count, :] = total[:, h * cols : (h + 1) * cols]


def shards(integrals, block_mask, green_occ, green_virt):
    auxs, total, _ = integrals.shape
    cols = green_virt.shape[1]
    tens_count = lax.axis_size("tens")
    rep_count = lax.axis_size("rep")
    mat_count = lax.axis_size("mat")
    owners = tens_count * rep_count
    kinds = 2 * auxs
    parts = owners // cols
    lanes = total // parts

    hbm = pl.BlockSpec(memory_space=pltpu.HBM)
    send = pl.pallas_call(
        dress_kernel,
        out_shape=jax.ShapeDtypeStruct((parts, cols * kinds, lanes), BF),
        in_specs=[hbm] * 4,
        scratch_shapes=[
            pltpu.VMEM(block_mask.shape, jnp.int32),
            pltpu.VMEM((2 * cols, total), BF),
            pltpu.VMEM((total, total), BF),
            pltpu.VMEM(integrals.shape, BF),
            pltpu.VMEM((auxs * cols, total), BF),
            pltpu.VMEM((kinds * cols, total), BF),
            pltpu.SemaphoreType.DMA((3 + auxs,)),
        ],
        compiler_params=LIMIT,
        name="dress",
    )(
        *[
            pltpu.with_memory_space_constraint(x, pltpu.HBM)
            for x in (block_mask, green_virt.T, green_occ, integrals)
        ]
    )

    got = lax.all_to_all(
        send.reshape(owners, kinds, lanes), ("tens", "rep"), 0, 0, tiled=True
    )

    folds = min(auxs, max(1, 128 // cols))
    partial = pl.pallas_call(
        lambda *refs: pair_kernel(tens_count, rep_count, folds, 1.0 / total, *refs),
        out_shape=jax.ShapeDtypeStruct((mat_count * rep_count, cols, tens_count * auxs), BF),
        compiler_params=LIMIT,
        name="pair",
    )(got.reshape(owners * kinds, lanes))
    partial = lax.all_to_all(partial, ("mat", "rep"), 0, 0, tiled=True)

    rows = pl.pallas_call(
        plane_kernel,
        out_shape=jax.ShapeDtypeStruct((tens_count * auxs // folds, folds * cols), F32),
        compiler_params=LIMIT,
        name="plane_sum",
    )(partial)
    rows = rows.reshape(tens_count, auxs // folds, folds * cols)
    rows = lax.all_to_all(rows, "tens", 0, 0, tiled=True)
    return pl.pallas_call(
        own_kernel,
        out_shape=jax.ShapeDtypeStruct((auxs, cols), F32),
        compiler_params=LIMIT,
        name="own_sum",
    )(rows)


def solution(mesh):
    return jax.shard_map(
        shards,
        mesh=mesh,
        in_specs=(
            P(("tens", "rep"), None, None),
            P(("tens", "rep"), None, None),
            P(),
            P(None, "mat"),
        ),
        out_specs=P(("tens", "rep"), "mat"),
        check_vma=False,
    )
```

```python
import jax
import jax.numpy as jnp
from jax import lax
from jax.experimental import pallas as pl
from jax.experimental.pallas import tpu as pltpu
from jax.sharding import PartitionSpec as P

BF = jnp.bfloat16
F32 = jnp.float32
NT = (((1,), (1,)), ((), ()))
LIMIT = pltpu.CompilerParams(vmem_limit_bytes=32 * 1024 * 1024)


def one_hot(rows, cols, column_of):
    row = lax.broadcasted_iota(jnp.int32, (rows, 1), 0)
    col = lax.broadcasted_iota(jnp.int32, (rows, cols), 1)
    return jnp.where(column_of(row) == col, 1.0, 0.0).astype(BF)


def dress_kernel(
    mask_hbm, virt_hbm, occ_hbm, slab_hbm, out_ref,
    mask_ref, left_ref, occ_ref, slab_ref, half_ref, rows_ref, sems,
):
    auxs, total, _ = slab_ref.shape
    blocks = mask_ref.shape[1]
    width = total // blocks
    cols = virt_hbm.shape[0]
    mask = pltpu.make_async_copy(mask_hbm, mask_ref, sems.at[0])
    virt = pltpu.make_async_copy(virt_hbm, left_ref.at[pl.ds(0, cols)], sems.at[1])
    occ = pltpu.make_async_copy(occ_hbm, occ_ref, sems.at[2])
    slabs = [
        pltpu.make_async_copy(slab_hbm.at[a], slab_ref.at[a], sems.at[3 + a]) for a in range(auxs)
    ]
    for copy in slabs[:1] + [mask, virt] + slabs[1:] + [occ]:
        copy.start()

    start = lax.axis_index("mat") * cols
    left_ref[cols:, :] = one_hot(cols, total, lambda row: row + start)
    kinds = rows_ref.shape[0] // cols
    band = min(cols, 32)
    order = one_hot(
        kinds * band, kinds * band, lambda row: (row % kinds) * band + row // kinds
    )
    lane_block = lax.broadcasted_iota(jnp.int32, (1, total), 1) // width

    mask.wait()
    factors = []
    for a in range(auxs):
        for row in range(blocks):
            kept = mask_ref[a, row : row + 1, :].astype(F32)
            factor = jnp.zeros((1, total), F32)
            for c in range(blocks):
                factor = jnp.where(lane_block == c, kept[:, c : c + 1], factor)
            factors.append(factor.astype(BF))
    virt.wait()
    for a in range(auxs):
        slabs[a].wait()
        for b in range(0, blocks, 2):
            strips = []
            for row in (b, b + 1):
                strip = slab_ref[a, row * width : (row + 1) * width, :]
                strips.append(strip * factors[a * blocks + row])
            strip = jnp.concatenate(strips, axis=0)
            at = slice(b * width, (b + 2) * width)
            both = lax.dot_general(left_ref[...], strip, NT, preferred_element_type=F32).astype(BF)
            half_ref[a * cols : (a + 1) * cols, at] = both[:cols]
            rows_ref[(auxs + a) * cols : (auxs + a + 1) * cols, at] = both[cols:]
    occ.wait()
    rows_ref[: auxs * cols, :] = jnp.dot(
        half_ref[...], occ_ref[...], preferred_element_type=F32
    ).astype(BF)

    parts, lanes = out_ref.shape[0], out_ref.shape[2]
    for h in range(parts):
        for g in range(cols // band):
            rows = jnp.concatenate(
                [
                    rows_ref[
                        j * cols + g * band : j * cols + (g + 1) * band,
                        h * lanes : (h + 1) * lanes,
                    ]
                    for j in range(kinds)
                ],
                axis=0,
            )
            out_ref[h, g * kinds * band : (g + 1) * kinds * band, :] = jnp.dot(
                order, rows, preferred_element_type=F32
            ).astype(BF)


def pair_kernel(tens_count, rep_count, folds, scale, got_ref, out_ref):
    height = got_ref.shape[0]
    kinds = height // (tens_count * rep_count)
    aux = kinds // 2
    low_count = aux // folds
    near = min(tens_count, max(1, 256 // (rep_count * kinds)))
    rows = near * rep_count * kinds
    piece = near * low_count

    def source_row(row):
        r, rest = row // (near * aux), row % (near * aux)
        high, rest = rest // piece, rest % piece
        t, low = rest // low_count, rest % low_count
        dressed = (t * rep_count + r) * kinds + high * low_count + low
        back = row - rows // 2
        masked = (back // aux) * kinds + aux + back % aux
        return jnp.where(row < rows // 2, dressed, masked)

    order = one_hot(rows, rows, source_row)
    groups = [
        jnp.dot(
            order, got_ref[g * rows : (g + 1) * rows, :], preferred_element_type=F32
        ).astype(BF)
        for g in range(height // rows)
    ]
    dressed = jnp.concatenate(
        [
            group[(r * folds + high) * piece : (r * folds + high + 1) * piece]
            for r in range(rep_count)
            for high in range(folds)
            for group in groups
        ],
        axis=0,
    )
    slots, cols, lanes = out_ref.shape
    for g, group in enumerate(groups):
        block = lax.dot_general(group[rows // 2 :], dressed, NT, preferred_element_type=F32)
        block = (block * scale).astype(out_ref.dtype)
        per = block.shape[0] // cols
        for k in range(per):
            for r in range(rep_count):
                out_ref[(g * per + k) * rep_count + r] = block[
                    k * cols : (k + 1) * cols, r * lanes : (r + 1) * lanes
                ]


def plane_kernel(got_ref, out_ref):
    total = got_ref[0].astype(F32)
    for k in range(1, got_ref.shape[0]):
        total = total + got_ref[k].astype(F32)
    rows = out_ref.shape[0]
    folds = total.shape[1] // rows
    out_ref[...] = jnp.concatenate(
        [total[:, h * rows : (h + 1) * rows].T for h in range(folds)], axis=1
    )


def own_kernel(got_ref, out_ref):
    total = got_ref[0]
    for k in range(1, got_ref.shape[0]):
        total = total + got_ref[k]
    low_count = total.shape[0]
    auxs, cols = out_ref.shape
    for h in range(auxs // low_count):
        out_ref[h * low_count : (h + 1) * low_count, :] = total[:, h * cols : (h + 1) * cols]


def shards(integrals, block_mask, green_occ, green_virt):
    auxs, total, _ = integrals.shape
    cols = green_virt.shape[1]
    tens_count = lax.axis_size("tens")
    rep_count = lax.axis_size("rep")
    mat_count = lax.axis_size("mat")
    owners = tens_count * rep_count
    kinds = 2 * auxs
    parts = owners // cols
    lanes = total // parts

    hbm = pl.BlockSpec(memory_space=pltpu.HBM)
    send = pl.pallas_call(
        dress_kernel,
        out_shape=jax.ShapeDtypeStruct((parts, cols * kinds, lanes), BF),
        in_specs=[hbm] * 4,
        scratch_shapes=[
            pltpu.VMEM(block_mask.shape, jnp.int32),
            pltpu.VMEM((2 * cols, total), BF),
            pltpu.VMEM((total, total), BF),
            pltpu.VMEM(integrals.shape, BF),
            pltpu.VMEM((auxs * cols, total), BF),
            pltpu.VMEM((kinds * cols, total), BF),
            pltpu.SemaphoreType.DMA((3 + auxs,)),
        ],
        compiler_params=LIMIT,
        name="dress",
    )(
        *[
            pltpu.with_memory_space_constraint(x, pltpu.HBM)
            for x in (block_mask, green_virt.T, green_occ, integrals)
        ]
    )

    got = lax.all_to_all(
        send.reshape(owners, kinds, lanes), ("tens", "rep"), 0, 0, tiled=True
    )

    folds = min(auxs, max(1, 128 // cols))
    partial = pl.pallas_call(
        lambda *refs: pair_kernel(tens_count, rep_count, folds, 1.0 / total, *refs),
        out_shape=jax.ShapeDtypeStruct((mat_count * rep_count, cols, tens_count * auxs), F32),
        compiler_params=LIMIT,
        name="pair",
    )(got.reshape(owners * kinds, lanes))
    partial = lax.all_to_all(partial, ("mat", "rep"), 0, 0, tiled=True)

    rows = pl.pallas_call(
        plane_kernel,
        out_shape=jax.ShapeDtypeStruct((tens_count * auxs // folds, folds * cols), F32),
        compiler_params=LIMIT,
        name="plane_sum",
    )(partial)
    rows = rows.reshape(tens_count, auxs // folds, folds * cols)
    rows = lax.all_to_all(rows, "tens", 0, 0, tiled=True)
    return pl.pallas_call(
        own_kernel,
        out_shape=jax.ShapeDtypeStruct((auxs, cols), F32),
        compiler_params=LIMIT,
        name="own_sum",
    )(rows)


def solution(mesh):
    return jax.shard_map(
        shards,
        mesh=mesh,
        in_specs=(
            P(("tens", "rep"), None, None),
            P(("tens", "rep"), None, None),
            P(),
            P(None, "mat"),
        ),
        out_specs=P(("tens", "rep"), "mat"),
        check_vma=False,
    )
```

```python
import jax
import jax.numpy as jnp
from jax import lax
from jax.experimental import pallas as pl
from jax.experimental.pallas import tpu as pltpu
from jax.sharding import PartitionSpec as P

BF = jnp.bfloat16
F32 = jnp.float32
NT = (((1,), (1,)), ((), ()))
LIMIT = pltpu.CompilerParams(vmem_limit_bytes=32 * 1024 * 1024)


def one_hot(rows, cols, column_of):
    row = lax.broadcasted_iota(jnp.int32, (rows, 1), 0)
    col = lax.broadcasted_iota(jnp.int32, (rows, cols), 1)
    return jnp.where(column_of(row) == col, 1.0, 0.0).astype(BF)


def dress_kernel(
    mask_hbm, virt_hbm, occ_hbm, slab_hbm, out_ref,
    mask_ref, left_ref, occ_ref, slab_ref, half_ref, rows_ref, sems,
):
    auxs, total, _ = slab_ref.shape
    blocks = mask_ref.shape[1]
    width = total // blocks
    cols = virt_hbm.shape[0]
    mask = pltpu.make_async_copy(mask_hbm, mask_ref, sems.at[0])
    virt = pltpu.make_async_copy(virt_hbm, left_ref.at[pl.ds(0, cols)], sems.at[1])
    occ = pltpu.make_async_copy(occ_hbm, occ_ref, sems.at[2])
    slabs = [
        pltpu.make_async_copy(slab_hbm.at[a], slab_ref.at[a], sems.at[3 + a]) for a in range(auxs)
    ]
    for copy in slabs[:1] + [mask, virt] + slabs[1:] + [occ]:
        copy.start()

    start = lax.axis_index("mat") * cols
    left_ref[cols:, :] = one_hot(cols, total, lambda row: row + start)
    kinds = rows_ref.shape[0] // cols
    band = min(cols, 32)
    order = one_hot(
        kinds * band, kinds * band, lambda row: (row % kinds) * band + row // kinds
    )
    lane_block = lax.broadcasted_iota(jnp.int32, (1, total), 1) // width

    mask.wait()
    factors = []
    for a in range(auxs):
        for row in range(blocks):
            kept = mask_ref[a, row : row + 1, :].astype(F32)
            factor = jnp.zeros((1, total), F32)
            for c in range(blocks):
                factor = jnp.where(lane_block == c, kept[:, c : c + 1], factor)
            factors.append(factor.astype(BF))
    virt.wait()
    for a in range(auxs):
        slabs[a].wait()
        for b in range(0, blocks, 2):
            strips = []
            for row in (b, b + 1):
                strip = slab_ref[a, row * width : (row + 1) * width, :]
                strips.append(strip * factors[a * blocks + row])
            strip = jnp.concatenate(strips, axis=0)
            at = slice(b * width, (b + 2) * width)
            both = lax.dot_general(left_ref[...], strip, NT, preferred_element_type=F32).astype(BF)
            half_ref[a * cols : (a + 1) * cols, at] = both[:cols]
            rows_ref[(auxs + a) * cols : (auxs + a + 1) * cols, at] = both[cols:]
    occ.wait()
    rows_ref[: auxs * cols, :] = jnp.dot(
        half_ref[...], occ_ref[...], preferred_element_type=F32
    ).astype(BF)

    parts, lanes = out_ref.shape[0], out_ref.shape[2]
    for h in range(parts):
        for g in range(cols // band):
            rows = jnp.concatenate(
                [
                    rows_ref[
                        j * cols + g * band : j * cols + (g + 1) * band,
                        h * lanes : (h + 1) * lanes,
                    ]
                    for j in range(kinds)
                ],
                axis=0,
            )
            out_ref[h, g * kinds * band : (g + 1) * kinds * band, :] = jnp.dot(
                order, rows, preferred_element_type=F32
            ).astype(BF)


def pair_kernel(tens_count, rep_count, folds, scale, got_ref, out_ref):
    height = got_ref.shape[0]
    kinds = height // (tens_count * rep_count)
    aux = kinds // 2
    low_count = aux // folds
    near = min(tens_count, max(1, 256 // (rep_count * kinds)))
    rows = near * rep_count * kinds
    piece = near * low_count

    def source_row(row):
        r, rest = row // (near * aux), row % (near * aux)
        high, rest = rest // piece, rest % piece
        t, low = rest // low_count, rest % low_count
        dressed = (t * rep_count + r) * kinds + high * low_count + low
        back = row - rows // 2
        masked = (back // aux) * kinds + aux + back % aux
        return jnp.where(row < rows // 2, dressed, masked)

    order = one_hot(rows, rows, source_row)
    groups = [
        jnp.dot(
            order, got_ref[g * rows : (g + 1) * rows, :], preferred_element_type=F32
        ).astype(BF)
        for g in range(height // rows)
    ]
    dressed = jnp.concatenate(
        [
            group[(r * folds + high) * piece : (r * folds + high + 1) * piece]
            for r in range(rep_count)
            for high in range(folds)
            for group in groups
        ],
        axis=0,
    )
    slots, cols, lanes = out_ref.shape
    masked = jnp.concatenate([group[rows // 2 :] for group in groups], axis=0)
    block = lax.dot_general(masked, dressed, NT, preferred_element_type=F32)
    block = (block * scale).astype(out_ref.dtype)
    for k in range(slots // rep_count):
        for r in range(rep_count):
            out_ref[k * rep_count + r] = block[
                k * cols : (k + 1) * cols, r * lanes : (r + 1) * lanes
            ]


def plane_kernel(got_ref, out_ref):
    total = got_ref[0].astype(F32)
    for k in range(1, got_ref.shape[0]):
        total = total + got_ref[k].astype(F32)
    rows = out_ref.shape[0]
    folds = total.shape[1] // rows
    out_ref[...] = jnp.concatenate(
        [total[:, h * rows : (h + 1) * rows].T for h in range(folds)], axis=1
    )


def own_kernel(got_ref, out_ref):
    total = got_ref[0]
    for k in range(1, got_ref.shape[0]):
        total = total + got_ref[k]
    low_count = total.shape[0]
    auxs, cols = out_ref.shape
    for h in range(auxs // low_count):
        out_ref[h * low_count : (h + 1) * low_count, :] = total[:, h * cols : (h + 1) * cols]


def shards(integrals, block_mask, green_occ, green_virt):
    auxs, total, _ = integrals.shape
    cols = green_virt.shape[1]
    tens_count = lax.axis_size("tens")
    rep_count = lax.axis_size("rep")
    mat_count = lax.axis_size("mat")
    owners = tens_count * rep_count
    kinds = 2 * auxs
    parts = owners // cols
    lanes = total // parts

    hbm = pl.BlockSpec(memory_space=pltpu.HBM)
    send = pl.pallas_call(
        dress_kernel,
        out_shape=jax.ShapeDtypeStruct((parts, cols * kinds, lanes), BF),
        in_specs=[hbm] * 4,
        scratch_shapes=[
            pltpu.VMEM(block_mask.shape, jnp.int32),
            pltpu.VMEM((2 * cols, total), BF),
            pltpu.VMEM((total, total), BF),
            pltpu.VMEM(integrals.shape, BF),
            pltpu.VMEM((auxs * cols, total), BF),
            pltpu.VMEM((kinds * cols, total), BF),
            pltpu.SemaphoreType.DMA((3 + auxs,)),
        ],
        compiler_params=LIMIT,
        name="dress",
    )(
        *[
            pltpu.with_memory_space_constraint(x, pltpu.HBM)
            for x in (block_mask, green_virt.T, green_occ, integrals)
        ]
    )

    got = lax.all_to_all(
        send.reshape(owners, kinds, lanes), ("tens", "rep"), 0, 0, tiled=True
    )

    folds = min(auxs, max(1, 128 // cols))
    partial = pl.pallas_call(
        lambda *refs: pair_kernel(tens_count, rep_count, folds, 1.0 / total, *refs),
        out_shape=jax.ShapeDtypeStruct((mat_count * rep_count, cols, tens_count * auxs), BF),
        compiler_params=LIMIT,
        name="pair",
    )(got.reshape(owners * kinds, lanes))
    partial = lax.all_to_all(partial, ("mat", "rep"), 0, 0, tiled=True)

    rows = pl.pallas_call(
        plane_kernel,
        out_shape=jax.ShapeDtypeStruct((tens_count * auxs // folds, folds * cols), F32),
        compiler_params=LIMIT,
        name="plane_sum",
    )(partial)
    rows = rows.reshape(tens_count, auxs // folds, folds * cols)
    rows = lax.all_to_all(rows, "tens", 0, 0, tiled=True)
    return pl.pallas_call(
        own_kernel,
        out_shape=jax.ShapeDtypeStruct((auxs, cols), F32),
        compiler_params=LIMIT,
        name="own_sum",
    )(rows)


def solution(mesh):
    return jax.shard_map(
        shards,
        mesh=mesh,
        in_specs=(
            P(("tens", "rep"), None, None),
            P(("tens", "rep"), None, None),
            P(),
            P(None, "mat"),
        ),
        out_specs=P(("tens", "rep"), "mat"),
        check_vma=False,
    )
```

```python
import jax
import jax.numpy as jnp
from jax import lax
from jax.experimental import pallas as pl
from jax.experimental.pallas import tpu as pltpu
from jax.sharding import PartitionSpec as P

BF = jnp.bfloat16
F32 = jnp.float32
NT = (((1,), (1,)), ((), ()))
LIMIT = pltpu.CompilerParams(vmem_limit_bytes=32 * 1024 * 1024)


def one_hot(rows, cols, column_of):
    row = lax.broadcasted_iota(jnp.int32, (rows, 1), 0)
    col = lax.broadcasted_iota(jnp.int32, (rows, cols), 1)
    return jnp.where(column_of(row) == col, 1.0, 0.0).astype(BF)


def dress_kernel(
    mask_hbm, virt_hbm, occ_hbm, slab_hbm, out_ref,
    mask_ref, left_ref, occ_ref, slab_ref, half_ref, rows_ref, sems,
):
    auxs, total, _ = slab_ref.shape
    blocks = mask_ref.shape[1]
    width = total // blocks
    cols = virt_hbm.shape[0]
    mask = pltpu.make_async_copy(mask_hbm, mask_ref, sems.at[0])
    virt = pltpu.make_async_copy(virt_hbm, left_ref.at[pl.ds(0, cols)], sems.at[1])
    occ = pltpu.make_async_copy(occ_hbm, occ_ref, sems.at[2])
    slabs = [
        pltpu.make_async_copy(slab_hbm.at[a], slab_ref.at[a], sems.at[3 + a]) for a in range(auxs)
    ]
    for copy in slabs[:1] + [mask, virt] + slabs[1:] + [occ]:
        copy.start()

    start = lax.axis_index("mat") * cols
    left_ref[cols:, :] = one_hot(cols, total, lambda row: row + start)
    kinds = rows_ref.shape[0] // cols
    band = min(cols, 32)
    order = one_hot(
        kinds * band, kinds * band, lambda row: (row % kinds) * band + row // kinds
    )
    lane_block = lax.broadcasted_iota(jnp.int32, (1, total), 1) // width

    mask.wait()
    factors = []
    for a in range(auxs):
        for row in range(blocks):
            kept = mask_ref[a, row : row + 1, :].astype(F32)
            factor = jnp.zeros((1, total), F32)
            for c in range(blocks):
                factor = jnp.where(lane_block == c, kept[:, c : c + 1], factor)
            factors.append(factor.astype(BF))
    virt.wait()
    for a in range(auxs):
        slabs[a].wait()
        for b in range(0, blocks, 2):
            strips = []
            for row in (b, b + 1):
                strip = slab_ref[a, row * width : (row + 1) * width, :]
                strips.append(strip * factors[a * blocks + row])
            strip = jnp.concatenate(strips, axis=0)
            at = slice(b * width, (b + 2) * width)
            both = lax.dot_general(left_ref[...], strip, NT, preferred_element_type=F32).astype(BF)
            half_ref[a * cols : (a + 1) * cols, at] = both[:cols]
            rows_ref[(auxs + a) * cols : (auxs + a + 1) * cols, at] = both[cols:]
    occ.wait()
    parts, lanes = out_ref.shape[0], out_ref.shape[2]
    for h in range(parts):
        at = slice(h * lanes, (h + 1) * lanes)
        rows_ref[: auxs * cols, at] = jnp.dot(
            half_ref[...], occ_ref[:, at], preferred_element_type=F32
        ).astype(BF)
        for g in range(cols // band):
            rows = jnp.concatenate(
                [
                    rows_ref[
                        j * cols + g * band : j * cols + (g + 1) * band,
                        h * lanes : (h + 1) * lanes,
                    ]
                    for j in range(kinds)
                ],
                axis=0,
            )
            out_ref[h, g * kinds * band : (g + 1) * kinds * band, :] = jnp.dot(
                order, rows, preferred_element_type=F32
            ).astype(BF)


def pair_kernel(tens_count, rep_count, folds, scale, got_ref, out_ref):
    height = got_ref.shape[0]
    kinds = height // (tens_count * rep_count)
    aux = kinds // 2
    low_count = aux // folds
    near = min(tens_count, max(1, 256 // (rep_count * kinds)))
    rows = near * rep_count * kinds
    piece = near * low_count

    def source_row(row):
        r, rest = row // (near * aux), row % (near * aux)
        high, rest = rest // piece, rest % piece
        t, low = rest // low_count, rest % low_count
        dressed = (t * rep_count + r) * kinds + high * low_count + low
        back = row - rows // 2
        masked = (back // aux) * kinds + aux + back % aux
        return jnp.where(row < rows // 2, dressed, masked)

    order = one_hot(rows, rows, source_row)
    groups = [
        jnp.dot(
            order, got_ref[g * rows : (g + 1) * rows, :], preferred_element_type=F32
        ).astype(BF)
        for g in range(height // rows)
    ]
    dressed = jnp.concatenate(
        [
            group[(r * folds + high) * piece : (r * folds + high + 1) * piece]
            for r in range(rep_count)
            for high in range(folds)
            for group in groups
        ],
        axis=0,
    )
    slots, cols, lanes = out_ref.shape
    masked = jnp.concatenate([group[rows // 2 :] for group in groups], axis=0)
    block = lax.dot_general(masked, dressed, NT, preferred_element_type=F32)
    block = (block * scale).astype(out_ref.dtype)
    for k in range(slots // rep_count):
        for r in range(rep_count):
            out_ref[k * rep_count + r] = block[
                k * cols : (k + 1) * cols, r * lanes : (r + 1) * lanes
            ]


def plane_kernel(got_ref, out_ref):
    total = got_ref[0].astype(F32)
    for k in range(1, got_ref.shape[0]):
        total = total + got_ref[k].astype(F32)
    rows = out_ref.shape[0]
    folds = total.shape[1] // rows
    out_ref[...] = jnp.concatenate(
        [total[:, h * rows : (h + 1) * rows].T for h in range(folds)], axis=1
    )


def own_kernel(got_ref, out_ref):
    total = got_ref[0]
    for k in range(1, got_ref.shape[0]):
        total = total + got_ref[k]
    low_count = total.shape[0]
    auxs, cols = out_ref.shape
    for h in range(auxs // low_count):
        out_ref[h * low_count : (h + 1) * low_count, :] = total[:, h * cols : (h + 1) * cols]


def shards(integrals, block_mask, green_occ, green_virt):
    auxs, total, _ = integrals.shape
    cols = green_virt.shape[1]
    tens_count = lax.axis_size("tens")
    rep_count = lax.axis_size("rep")
    mat_count = lax.axis_size("mat")
    owners = tens_count * rep_count
    kinds = 2 * auxs
    parts = owners // cols
    lanes = total // parts

    hbm = pl.BlockSpec(memory_space=pltpu.HBM)
    send = pl.pallas_call(
        dress_kernel,
        out_shape=jax.ShapeDtypeStruct((parts, cols * kinds, lanes), BF),
        in_specs=[hbm] * 4,
        scratch_shapes=[
            pltpu.VMEM(block_mask.shape, jnp.int32),
            pltpu.VMEM((2 * cols, total), BF),
            pltpu.VMEM((total, total), BF),
            pltpu.VMEM(integrals.shape, BF),
            pltpu.VMEM((auxs * cols, total), BF),
            pltpu.VMEM((kinds * cols, total), BF),
            pltpu.SemaphoreType.DMA((3 + auxs,)),
        ],
        compiler_params=LIMIT,
        name="dress",
    )(
        *[
            pltpu.with_memory_space_constraint(x, pltpu.HBM)
            for x in (block_mask, green_virt.T, green_occ, integrals)
        ]
    )

    got = lax.all_to_all(
        send.reshape(owners, kinds, lanes), ("tens", "rep"), 0, 0, tiled=True
    )

    folds = min(auxs, max(1, 128 // cols))
    partial = pl.pallas_call(
        lambda *refs: pair_kernel(tens_count, rep_count, folds, 1.0 / total, *refs),
        out_shape=jax.ShapeDtypeStruct((mat_count * rep_count, cols, tens_count * auxs), BF),
        compiler_params=LIMIT,
        name="pair",
    )(got.reshape(owners * kinds, lanes))
    partial = lax.all_to_all(partial, ("mat", "rep"), 0, 0, tiled=True)

    rows = pl.pallas_call(
        plane_kernel,
        out_shape=jax.ShapeDtypeStruct((tens_count * auxs // folds, folds * cols), F32),
        compiler_params=LIMIT,
        name="plane_sum",
    )(partial)
    rows = rows.reshape(tens_count, auxs // folds, folds * cols)
    rows = lax.all_to_all(rows, "tens", 0, 0, tiled=True)
    return pl.pallas_call(
        own_kernel,
        out_shape=jax.ShapeDtypeStruct((auxs, cols), F32),
        compiler_params=LIMIT,
        name="own_sum",
    )(rows)


def solution(mesh):
    return jax.shard_map(
        shards,
        mesh=mesh,
        in_specs=(
            P(("tens", "rep"), None, None),
            P(("tens", "rep"), None, None),
            P(),
            P(None, "mat"),
        ),
        out_specs=P(("tens", "rep"), "mat"),
        check_vma=False,
    )
```

```python
import jax
import jax.numpy as jnp
from jax import lax
from jax.experimental import pallas as pl
from jax.experimental.pallas import tpu as pltpu
from jax.sharding import PartitionSpec as P

BF = jnp.bfloat16
F32 = jnp.float32
NT = (((1,), (1,)), ((), ()))
LIMIT = pltpu.CompilerParams(vmem_limit_bytes=32 * 1024 * 1024)


def one_hot(rows, cols, column_of):
    row = lax.broadcasted_iota(jnp.int32, (rows, 1), 0)
    col = lax.broadcasted_iota(jnp.int32, (rows, cols), 1)
    return jnp.where(column_of(row) == col, 1.0, 0.0).astype(BF)


def dress_kernel(
    mask_hbm, virt_hbm, occ_hbm, slab_hbm, out_ref,
    mask_ref, left_ref, occ_ref, slab_ref, half_ref, rows_ref, sems,
):
    auxs, total, _ = slab_ref.shape
    blocks = mask_ref.shape[1]
    width = total // blocks
    cols = virt_hbm.shape[0]
    mask = pltpu.make_async_copy(mask_hbm, mask_ref, sems.at[0])
    virt = pltpu.make_async_copy(virt_hbm, left_ref.at[pl.ds(0, cols)], sems.at[1])
    occ = pltpu.make_async_copy(occ_hbm, occ_ref, sems.at[2])
    slabs = [
        pltpu.make_async_copy(slab_hbm.at[a], slab_ref.at[a], sems.at[3 + a]) for a in range(auxs)
    ]
    for copy in slabs[:1] + [mask, virt] + slabs[1:] + [occ]:
        copy.start()

    start = lax.axis_index("mat") * cols
    left_ref[cols:, :] = one_hot(cols, total, lambda row: row + start)
    kinds = rows_ref.shape[0] // cols
    band = min(cols, 16)
    order = one_hot(
        kinds * band, kinds * band, lambda row: (row % kinds) * band + row // kinds
    )
    lane_block = lax.broadcasted_iota(jnp.int32, (1, total), 1) // width

    mask.wait()
    factors = []
    for a in range(auxs):
        for row in range(blocks):
            kept = mask_ref[a, row : row + 1, :].astype(F32)
            factor = jnp.zeros((1, total), F32)
            for c in range(blocks):
                factor = jnp.where(lane_block == c, kept[:, c : c + 1], factor)
            factors.append(factor.astype(BF))
    virt.wait()
    for a in range(auxs):
        slabs[a].wait()
        for b in range(0, blocks, 2):
            strips = []
            for row in (b, b + 1):
                strip = slab_ref[a, row * width : (row + 1) * width, :]
                strips.append(strip * factors[a * blocks + row])
            strip = jnp.concatenate(strips, axis=0)
            at = slice(b * width, (b + 2) * width)
            both = lax.dot_general(left_ref[...], strip, NT, preferred_element_type=F32).astype(BF)
            half_ref[a * cols : (a + 1) * cols, at] = both[:cols]
            rows_ref[(auxs + a) * cols : (auxs + a + 1) * cols, at] = both[cols:]
    occ.wait()
    rows_ref[: auxs * cols, :] = jnp.dot(
        half_ref[...], occ_ref[...], preferred_element_type=F32
    ).astype(BF)

    parts, lanes = out_ref.shape[0], out_ref.shape[2]
    for h in range(parts):
        for g in range(cols // band):
            rows = jnp.concatenate(
                [
                    rows_ref[
                        j * cols + g * band : j * cols + (g + 1) * band,
                        h * lanes : (h + 1) * lanes,
                    ]
                    for j in range(kinds)
                ],
                axis=0,
            )
            out_ref[h, g * kinds * band : (g + 1) * kinds * band, :] = jnp.dot(
                order, rows, preferred_element_type=F32
            ).astype(BF)


def pair_kernel(tens_count, rep_count, folds, scale, got_ref, out_ref):
    height = got_ref.shape[0]
    kinds = height // (tens_count * rep_count)
    aux = kinds // 2
    low_count = aux // folds
    near = min(tens_count, max(1, 256 // (rep_count * kinds)))
    rows = near * rep_count * kinds
    piece = near * low_count

    def source_row(row):
        r, rest = row // (near * aux), row % (near * aux)
        high, rest = rest // piece, rest % piece
        t, low = rest // low_count, rest % low_count
        dressed = (t * rep_count + r) * kinds + high * low_count + low
        back = row - rows // 2
        masked = (back // aux) * kinds + aux + back % aux
        return jnp.where(row < rows // 2, dressed, masked)

    order = one_hot(rows, rows, source_row)
    groups = [
        jnp.dot(
            order, got_ref[g * rows : (g + 1) * rows, :], preferred_element_type=F32
        ).astype(BF)
        for g in range(height // rows)
    ]
    dressed = jnp.concatenate(
        [
            group[(r * folds + high) * piece : (r * folds + high + 1) * piece]
            for r in range(rep_count)
            for high in range(folds)
            for group in groups
        ],
        axis=0,
    )
    slots, cols, lanes = out_ref.shape
    for g, group in enumerate(groups):
        block = lax.dot_general(group[rows // 2 :], dressed, NT, preferred_element_type=F32)
        block = (block * scale).astype(out_ref.dtype)
        per = block.shape[0] // cols
        for k in range(per):
            for r in range(rep_count):
                out_ref[(g * per + k) * rep_count + r] = block[
                    k * cols : (k + 1) * cols, r * lanes : (r + 1) * lanes
                ]


def plane_kernel(got_ref, out_ref):
    total = got_ref[0].astype(F32)
    for k in range(1, got_ref.shape[0]):
        total = total + got_ref[k].astype(F32)
    rows = out_ref.shape[0]
    folds = total.shape[1] // rows
    out_ref[...] = jnp.concatenate(
        [total[:, h * rows : (h + 1) * rows].T for h in range(folds)], axis=1
    )


def own_kernel(got_ref, out_ref):
    total = got_ref[0]
    for k in range(1, got_ref.shape[0]):
        total = total + got_ref[k]
    low_count = total.shape[0]
    auxs, cols = out_ref.shape
    for h in range(auxs // low_count):
        out_ref[h * low_count : (h + 1) * low_count, :] = total[:, h * cols : (h + 1) * cols]


def shards(integrals, block_mask, green_occ, green_virt):
    auxs, total, _ = integrals.shape
    cols = green_virt.shape[1]
    tens_count = lax.axis_size("tens")
    rep_count = lax.axis_size("rep")
    mat_count = lax.axis_size("mat")
    owners = tens_count * rep_count
    kinds = 2 * auxs
    parts = owners // cols
    lanes = total // parts

    hbm = pl.BlockSpec(memory_space=pltpu.HBM)
    send = pl.pallas_call(
        dress_kernel,
        out_shape=jax.ShapeDtypeStruct((parts, cols * kinds, lanes), BF),
        in_specs=[hbm] * 4,
        scratch_shapes=[
            pltpu.VMEM(block_mask.shape, jnp.int32),
            pltpu.VMEM((2 * cols, total), BF),
            pltpu.VMEM((total, total), BF),
            pltpu.VMEM(integrals.shape, BF),
            pltpu.VMEM((auxs * cols, total), BF),
            pltpu.VMEM((kinds * cols, total), BF),
            pltpu.SemaphoreType.DMA((3 + auxs,)),
        ],
        compiler_params=LIMIT,
        name="dress",
    )(
        *[
            pltpu.with_memory_space_constraint(x, pltpu.HBM)
            for x in (block_mask, green_virt.T, green_occ, integrals)
        ]
    )

    got = lax.all_to_all(
        send.reshape(owners, kinds, lanes), ("tens", "rep"), 0, 0, tiled=True
    )

    folds = min(auxs, max(1, 128 // cols))
    partial = pl.pallas_call(
        lambda *refs: pair_kernel(tens_count, rep_count, folds, 1.0 / total, *refs),
        out_shape=jax.ShapeDtypeStruct((mat_count * rep_count, cols, tens_count * auxs), BF),
        compiler_params=LIMIT,
        name="pair",
    )(got.reshape(owners * kinds, lanes))
    partial = lax.all_to_all(partial, ("mat", "rep"), 0, 0, tiled=True)

    rows = pl.pallas_call(
        plane_kernel,
        out_shape=jax.ShapeDtypeStruct((tens_count * auxs // folds, folds * cols), F32),
        compiler_params=LIMIT,
        name="plane_sum",
    )(partial)
    rows = rows.reshape(tens_count, auxs // folds, folds * cols)
    rows = lax.all_to_all(rows, "tens", 0, 0, tiled=True)
    return pl.pallas_call(
        own_kernel,
        out_shape=jax.ShapeDtypeStruct((auxs, cols), F32),
        compiler_params=LIMIT,
        name="own_sum",
    )(rows)


def solution(mesh):
    return jax.shard_map(
        shards,
        mesh=mesh,
        in_specs=(
            P(("tens", "rep"), None, None),
            P(("tens", "rep"), None, None),
            P(),
            P(None, "mat"),
        ),
        out_specs=P(("tens", "rep"), "mat"),
        check_vma=False,
    )
```
